32 devices in a mesh: grp: 2 (over y), row: 4 (over x, core), col: 4 (over z).
Axes of the slice: x: 2, y: 2, z: 4, core: 2. Of those that a mesh axis runs over, the one named last changes fastest.
Arguments:
- keys: bfloat16 [4, 128, 8192], P('grp', None, 'row'), parts along dimension 0, may hold values from -6 to 6
- values: bfloat16 [4, 128, 8192], P('grp', None, 'row'), parts along dimension 0, may hold values from -6 to 6
- queries: bfloat16 [4, 128, 8192], P('grp', None, 'row'), parts along dimension 0, may hold values from -6 to 6
- memory_in: bfloat16 [8192, 32768], P('row', 'col'), may hold values from -0.0625 to 0.0625
- memory_out: bfloat16 [32768, 8192], P('col', 'row'), may hold values from -0.03125 to 0.03125
- rates: float32 [4, 2], P('grp'), parts along dimension 0, may hold values from 0.5 to 3
- momentum: float32 [2], P('grp'), parts along dimension 0, may hold values from 0.05 to 0.99
- decay: float32 [4], P('grp'), parts along dimension 0, may hold values from 0.05 to 0.4
- valid: int32 [4], P('grp'), parts along dimension 0, may hold values from 64 to 128
Outputs:
- recalled: bfloat16 [4, 128, 8192], P('grp', 'col', 'row'), parts along dimension 0
The draws below stay inside these ranges and needn't reach their ends.
There are 2 independent parts, one for each index of `grp`. The reference program is written for one: setup_inputs(seed, part) draws one part's arguments, and reference() takes and returns one part's arrays. A program takes and returns all parts, laid end to end along the dimension named above; an argument that names none is the same for every part. Nothing has to cross between parts.
All inputs are finite; a program needn't handle non-finite values.
Results may differ from the reference program's by a relative error of at most 0.035.
Values may be sent and summed in bfloat16 or wider, within the bound.
A program may use at most 576 MiB of HBM per device.

```python
import math
import jax
import jax.numpy as jnp
from jax import lax

D = 8192
HID = 32768
BLOCK = 128
NBLOCK = 2
N_ROW = 4
N_COL = 4


def levels(own_key, dims, split, smallest, top_value):
    factor_of, own = 1.0, jax.random.fold_in(own_key, 6)
    for position, shards_of in split:
        draws = jnp.exp(jax.random.uniform(jax.random.fold_in(own, position), (shards_of,), jnp.float32, smallest / len(split), top_value / len(split)))
        factor_of = factor_of * jnp.repeat(draws, dims[position] // shards_of).reshape([-1 if axis == position else 1 for axis in range(len(dims))])
    return factor_of


def gaussian(stream_key, extent, spread, bound, cuts=(), dtype=jnp.bfloat16):
    result = spread * jax.random.normal(stream_key, extent, jnp.float32)
    if cuts:
        result = result * levels(stream_key, extent, cuts, -0.22, 0.18)
    return jnp.clip(result, -bound, bound).astype(dtype)


def setup_inputs(seed: int = 0, part: int = 0) -> dict:
    key_list = jax.random.split(jax.random.key(seed), 10)
    own_keys = jax.random.split(jax.random.fold_in(key_list[9], part), 10)
    return {
        "keys": gaussian(own_keys[0], (NBLOCK, BLOCK, D), 1.0, 6.0, ((2, 4),)),
        "values": gaussian(own_keys[1], (NBLOCK, BLOCK, D), 1.0, 6.0, ((2, 4),)),
        "queries": gaussian(own_keys[2], (NBLOCK, BLOCK, D), 1.0, 6.0, ((2, 4),)),
        "memory_in": gaussian(key_list[3], (D, HID), D ** -0.5, 0.0625, ((0, 4), (1, 4))),
        "memory_out": gaussian(key_list[4], (HID, D), HID ** -0.5, 0.03125, ((0, 4), (1, 4))),
        "rates": jnp.clip(jnp.exp(jax.random.uniform(own_keys[5], (NBLOCK, 2), jnp.float32, math.log(0.5), math.log(3.0))), 0.5, 3.0),
        "momentum": jnp.clip(jax.random.uniform(own_keys[6], (NBLOCK - 1,), jnp.float32, 0.05, 0.99), 0.05, 0.99),
        "decay": jnp.clip(jax.random.uniform(own_keys[7], (NBLOCK,), jnp.float32, 0.05, 0.4), 0.05, 0.4),
        "valid": jax.random.randint(own_keys[8], (NBLOCK,), BLOCK // 2, BLOCK + 1).astype(jnp.int32),
    }


def silu_grad(pre):
    sig = jax.nn.sigmoid(pre)
    return sig * (1.0 + pre * (1.0 - sig))

def split_product(left, right, parts):
    width = left.shape[1] // parts
    total = jnp.zeros((left.shape[0], right.shape[1]), jnp.float32)
    for part_index in range(parts):
        piece = jnp.dot(left[:, part_index * width:(part_index + 1) * width], right[part_index * width:(part_index + 1) * width], preferred_element_type=jnp.float32)
        total = total + lax.optimization_barrier(piece.astype(jnp.bfloat16)).astype(jnp.float32)
    return total

def reference(keys, values, queries, memory_in, memory_out, rates, momentum, decay, valid):
    w_in = memory_in.astype(jnp.float32)
    w_out = memory_out.astype(jnp.float32)
    b_in = memory_in
    b_out = memory_out
    mom_in = jnp.zeros(w_in.shape, jnp.float32)
    mom_out = jnp.zeros(w_out.shape, jnp.float32)
    results = []
    for block_index in range(NBLOCK):
        key_block = keys[block_index]
        pre = split_product(key_block, b_in, N_ROW)
        act = jax.nn.silu(pre).astype(jnp.bfloat16)
        out = split_product(act, b_out, N_COL)
        live = (jnp.arange(BLOCK) < valid[block_index]).astype(jnp.float32)[:, None]
        error = ((out - values[block_index].astype(jnp.float32)) * live).astype(jnp.bfloat16)
        grad_out = jnp.dot(act.T, error, preferred_element_type=jnp.float32)
        back = split_product(error, b_out.T, N_ROW)
        delta = (back * silu_grad(pre)).astype(jnp.bfloat16)
        grad_in = jnp.dot(key_block.T, delta, preferred_element_type=jnp.float32)
        step_in = rates[block_index, 0] / math.sqrt(D * BLOCK)
        step_out = rates[block_index, 1] / HID
        if block_index == 0:
            mom_in = -step_in * grad_in
            mom_out = -step_out * grad_out
        else:
            mom_in = momentum[block_index - 1] * mom_in - step_in * grad_in
            mom_out = momentum[block_index - 1] * mom_out - step_out * grad_out
        w_in = (1.0 - decay[block_index]) * w_in + mom_in
        w_out = (1.0 - decay[block_index]) * w_out + mom_out
        b_in = w_in.astype(jnp.bfloat16)
        b_out = w_out.astype(jnp.bfloat16)
        query_act = jax.nn.silu(split_product(queries[block_index], b_in, N_ROW)).astype(jnp.bfloat16)
        results.append(split_product(query_act, b_out, N_COL).astype(jnp.bfloat16))
    return jnp.stack(results, axis=0)
```

```python
import math

import jax
import jax.numpy as jnp
from jax import lax
from jax.sharding import PartitionSpec as P

BF = jnp.bfloat16
F32 = jnp.float32


def silu_grad(pre):
    sig = jax.nn.sigmoid(pre)
    return sig * (1.0 + pre * (1.0 - sig))


def mm(a, b, dims=((1,), (0,))):
    return lax.dot_general(a, b, (dims, ((), ())), preferred_element_type=F32)


NT = ((1,), (1,))


def scatter_row(x):
    return lax.psum_scatter(x.astype(BF), "row", scatter_dimension=1, tiled=True).astype(F32)


def gather_row(x):
    return lax.all_gather(x, "row", axis=1, tiled=True)


def per_device(keys, values, queries, w_in, w_out, rates, momentum, decay, valid):
    n_row = lax.axis_size("row")
    n_col = lax.axis_size("col")
    tokens = keys.shape[1]
    width = keys.shape[2] * n_row
    hidden = w_in.shape[1] * n_col
    step_in = rates[:, 0] / math.sqrt(width * tokens)
    step_out = rates[:, 1] / hidden
    keep0 = 1.0 - decay[0]
    keep1 = 1.0 - decay[1]
    both = keep0 * keep1
    carry = keep1 + momentum[0]
    k0, k1, q0, q1 = keys[0], keys[1], queries[0], queries[1]

    pre0 = scatter_row(mm(k0, w_in))
    gram = jnp.stack([mm(q0, k0, NT), mm(k1, k0, NT), mm(q1, k0, NT), mm(q1, k1, NT)])
    gram = lax.psum(gram, "row")
    rest = scatter_row(mm(jnp.concatenate([k1, q0, q1], axis=0), w_in))
    sum_k1, sum_q0, sum_q1 = rest[:tokens], rest[tokens : 2 * tokens], rest[2 * tokens :]

    def corr(index, scale, delta):
        return mm((scale * gram[index]).astype(BF), delta)

    def error_of(part, block):
        total = lax.psum(part.astype(BF), "col").astype(F32)
        live = (jnp.arange(tokens) < valid[block]).astype(F32)[:, None]
        return ((total - values[block].astype(F32)) * live).astype(BF)

    act0 = gather_row(jax.nn.silu(pre0).astype(BF))
    err0 = error_of(mm(act0, w_out), 0)
    delta0 = (scatter_row(mm(err0, w_out, NT)) * silu_grad(pre0)).astype(BF)
    pre1 = keep0 * sum_k1 - corr(1, step_in[0], delta0)
    act1 = gather_row(jax.nn.silu(pre1).astype(BF))
    qpre0 = keep0 * sum_q0 - corr(0, step_in[0], delta0)
    qact0 = gather_row(jax.nn.silu(qpre0).astype(BF))
    out1 = keep0 * mm(act1, w_out) - mm((step_out[0] * mm(act1, act0, NT)).astype(BF), err0)
    err1 = error_of(out1, 1)
    read0 = keep0 * mm(qact0, w_out) - mm((step_out[0] * mm(qact0, act0, NT)).astype(BF), err0)
    res0 = lax.psum_scatter(read0.astype(BF), "col", scatter_dimension=0, tiled=True)
    back1 = keep0 * mm(err1, w_out, NT) - mm((step_out[0] * mm(err1, err0, NT)).astype(BF), act0)
    delta1 = (scatter_row(back1) * silu_grad(pre1)).astype(BF)
    qpre1 = both * sum_q1 - corr(2, carry * step_in[0], delta0) - corr(3, step_in[1], delta1)
    qact1 = gather_row(jax.nn.silu(qpre1).astype(BF))
    read1 = (
        both * mm(qact1, w_out)
        - mm((carry * step_out[0] * mm(qact1, act0, NT)).astype(BF), err0)
        - mm((step_out[1] * mm(qact1, act1, NT)).astype(BF), err1)
    )
    res1 = lax.psum_scatter(read1.astype(BF), "col", scatter_dimension=0, tiled=True)
    return jnp.stack([res0, res1], axis=0)


def solution(mesh):
    placed = (
        P("grp", None, "row"),
        P("grp", None, "row"),
        P("grp", None, "row"),
        P("row", "col"),
        P("col", "row"),
        P("grp", None),
        P("grp"),
        P("grp"),
        P("grp"),
    )
    return jax.shard_map(
        per_device, mesh=mesh, in_specs=placed, out_specs=P("grp", "col", "row"), check_vma=False
    )
```

```python
import functools
import math

import jax
import jax.numpy as jnp
from jax import lax
from jax.experimental import pallas as pl
from jax.experimental.pallas import tpu as pltpu
from jax.sharding import PartitionSpec as P

BF = jnp.bfloat16
F32 = jnp.float32
NT = ((1,), (1,))


def silu_grad(pre):
    sig = jax.nn.sigmoid(pre)
    return sig * (1.0 + pre * (1.0 - sig))


def silu(pre):
    return jax.nn.silu(pre).astype(BF)


def mm(a, b, dims=((1,), (0,))):
    return lax.dot_general(a, b, (dims, ((), ())), preferred_element_type=F32)


def stream_kernel(kind, steps, fixed, *refs):
    where_ref, x_ref, w_ref = refs[:3]
    if fixed:
        scale_ref, inner_ref, act_ref, o_ref, held, sems = refs[3:]
    else:
        o_ref, held, sems = refs[3:]
    tile = held.shape[2] if kind == "in" else held.shape[1]
    base = where_ref[0] * (steps * tile)

    def copy(t):
        span = pl.ds(pl.multiple_of(base + t * tile, tile), tile)
        source = w_ref.at[:, span] if kind == "in" else w_ref.at[span, :]
        return pltpu.make_async_copy(source, held.at[t], sems.at[t])

    for t in range(steps):
        copy(t).start()
    for t in range(steps):
        copy(t).wait()
        cols = slice(t * tile, (t + 1) * tile)
        if kind == "in":
            o_ref[:, cols] = mm(x_ref[...], held[t]).astype(o_ref.dtype)
        elif kind == "out":
            value = mm(x_ref[:, cols], held[t])
            o_ref[...] = value if t == 0 else o_ref[...] + value
        else:
            value = mm(x_ref[...], held[t], NT)
            if fixed:
                value = scale_ref[0] * value - mm(inner_ref[...], act_ref[:, cols])
            o_ref[:, cols] = value.astype(o_ref.dtype)


def product(kind, x, w, where, piece, fix=None):
    rows = x.shape[0]
    depth = w.shape[0] if kind == "in" else w.shape[1]
    tile = min(512, piece)
    steps = piece // tile
    shape, dtype = ((rows, depth), F32) if kind == "out" else ((rows, piece), BF)
    smem = pl.BlockSpec(memory_space=pltpu.SMEM)
    vmem = pl.BlockSpec(memory_space=pltpu.VMEM)
    args, specs = [where, x, w], [smem, vmem, pl.BlockSpec(memory_space=pl.ANY)]
    if fix is not None:
        args += [fix[0][None], fix[1], fix[2]]
        specs += [smem, vmem, vmem]
    return pl.pallas_call(
        functools.partial(stream_kernel, kind, steps, fix is not None),
        in_specs=specs,
        out_specs=vmem,
        out_shape=jax.ShapeDtypeStruct(shape, dtype),
        scratch_shapes=[
            pltpu.VMEM((steps, depth, tile) if kind == "in" else (steps, tile, depth), BF),
            pltpu.SemaphoreType.DMA((steps,)),
        ],
        compiler_params=pltpu.CompilerParams(vmem_limit_bytes=24 * 2**20),
        cost_estimate=pl.CostEstimate(
            flops=2 * rows * depth * piece, bytes_accessed=2 * depth * piece, transcendentals=0
        ),
    )(*args)


def in_product(x, w, where, piece):
    return product("in", x, w, where, piece)


def out_product(x, w, where):
    return product("out", x, w, where, x.shape[1])


def back_product(x, w, where, piece, fix=None):
    return product("back", x, w, where, piece, fix)


def after(value, others):
    return lax.optimization_barrier((value, others))[0]


def per_device(keys, values, queries, w_in, w_out, rates, momentum, decay, valid):
    n_row = lax.axis_size("row")
    n_col = lax.axis_size("col")
    n_x = n_row // 2
    tokens = keys.shape[1]
    width = keys.shape[2] * n_row
    hid = w_in.shape[1]
    piece = hid // n_row
    hidden = hid * n_col
    me = lax.axis_index("row")
    my_x, my_core = me // 2, me % 2
    my_col = lax.axis_index("col")
    step_in = rates[:, 0] / math.sqrt(width * tokens)
    step_out = rates[:, 1] / hidden
    keep0 = 1.0 - decay[0]
    keep1 = 1.0 - decay[1]
    both = keep0 * keep1
    carry = keep1 + momentum[0]
    k0, k1, q0, q1 = keys[0], keys[1], queries[0], queries[1]

    names = [(j, s) for s in (1, 0) for j in list(range(1, n_x)) + [0]]

    def number(name):
        j, s = name
        return ((my_x + j) % n_x) * 2 + (my_core + s) % 2

    where = {n: number(n)[None].astype(jnp.int32) for n in names}

    swap = [(i, i ^ 1) for i in range(n_row)]

    def along_x(value, j):
        return lax.ppermute(value, "row", [(i, (i + 2 * j) % n_row) for i in range(n_row)])

    def along_col(value, j):
        return lax.ppermute(value, "col", [(i, (i + j) % n_col) for i in range(n_col)])

    def scatter_row(parts):
        crossed = {j: lax.ppermute(parts[(j, 1)], "row", swap) for j in range(n_x)}
        chip = {j: parts[(j, 0)].astype(F32) + crossed[j].astype(F32) for j in range(n_x)}
        total = chip[0]
        for j in range(1, n_x):
            total = total + along_x(chip[j].astype(BF), j).astype(F32)
        return total

    def gather_row(mine):
        pieces = {(0, 0): mine}
        for j in range(1, n_x):
            pieces[(n_x - j, 0)] = along_x(mine, j)
        for j in range(n_x):
            pieces[(j, 1)] = lax.ppermute(pieces[(j, 0)], "row", swap)
        return pieces

    order = [(j, s) for s in (0, 1) for j in range(n_x)]

    def times_out(pieces):
        return sum(out_product(pieces[n], w_out, where[n]) for n in order)

    def gram_of(left, right):
        return sum(mm(left[n], right[n], NT) for n in order)

    rows = tokens // n_col

    def scatter_col(part):
        part = part.astype(BF)
        total = lax.dynamic_slice_in_dim(part, my_col * rows, rows, 0).astype(F32)
        for j in range(1, n_col):
            term = lax.dynamic_slice_in_dim(part, ((my_col + j) % n_col) * rows, rows, 0)
            total = total + along_col(term, j).astype(F32)
        return total

    def error_of(part, block):
        total = scatter_col(part)
        wanted = lax.dynamic_slice_in_dim(values[block], my_col * rows, rows, 0).astype(F32)
        live = ((my_col * rows + jnp.arange(rows)) < valid[block]).astype(F32)[:, None]
        error = ((total - wanted) * live).astype(BF)
        blocks = [error] + [along_col(error, j) for j in range(n_col - 1, 0, -1)]
        full = jnp.concatenate(blocks + blocks, axis=0)
        return lax.dynamic_slice_in_dim(full, ((n_col - my_col) % n_col) * rows, tokens, 0)

    pre_parts = {n: in_product(k0, w_in, where[n], piece) for n in names}
    others = after(jnp.concatenate([k1, q0, q1], axis=0), pre_parts)
    rest_parts = {n: in_product(others, w_in, where[n], piece) for n in names}
    pre0 = scatter_row(pre_parts)
    gram = jnp.stack([mm(q0, k0, NT), mm(k1, k0, NT), mm(q1, k0, NT), mm(q1, k1, NT)])
    gram = lax.psum(gram, "row")

    def corr(index, scale, delta):
        return mm((scale * gram[index]).astype(BF), delta)

    act0 = gather_row(silu(pre0))
    rest_parts = after(rest_parts, act0)
    sum_k1, sum_q0, sum_q1 = [
        scatter_row({n: rest_parts[n][i * tokens : (i + 1) * tokens] for n in names})
        for i in range(3)
    ]
    err0 = error_of(times_out(act0), 0)
    back0 = {n: back_product(err0, w_out, where[n], piece) for n in names}
    delta0 = (scatter_row(back0) * silu_grad(pre0)).astype(BF)
    pre1 = keep0 * sum_k1 - corr(1, step_in[0], delta0)
    act1 = gather_row(silu(pre1))
    qpre0 = keep0 * sum_q0 - corr(0, step_in[0], delta0)
    qact0 = gather_row(after(silu(qpre0), act1))
    out1 = keep0 * times_out(act1) - mm((step_out[0] * gram_of(act1, act0)).astype(BF), err0)
    err1 = error_of(out1, 1)
    qact0 = after(qact0, out1)
    read0 = keep0 * times_out(qact0) - mm((step_out[0] * gram_of(qact0, act0)).astype(BF), err0)
    inner = (step_out[0] * mm(err1, err0, NT)).astype(BF)
    back1 = {
        n: back_product(err1, w_out, where[n], piece, (keep0, inner, act0[n])) for n in names
    }
    delta1 = (scatter_row(back1) * silu_grad(pre1)).astype(BF)
    res0 = scatter_col(after(read0, back1)).astype(BF)
    qpre1 = both * sum_q1 - corr(2, carry * step_in[0], delta0) - corr(3, step_in[1], delta1)
    qact1 = gather_row(silu(qpre1))
    read1 = (
        both * times_out(qact1)
        - mm((carry * step_out[0] * gram_of(qact1, act0)).astype(BF), err0)
        - mm((step_out[1] * gram_of(qact1, act1)).astype(BF), err1)
    )
    res1 = scatter_col(read1).astype(BF)
    return jnp.stack([res0, res1], axis=0)


def solution(mesh):
    placed = (
        P("grp", None, "row"),
        P("grp", None, "row"),
        P("grp", None, "row"),
        P("row", "col"),
        P("col", "row"),
        P("grp", None),
        P("grp"),
        P("grp"),
        P("grp"),
    )
    return jax.shard_map(
        per_device, mesh=mesh, in_specs=placed, out_specs=P("grp", "col", "row"), check_vma=False
    )
```
